1024 devices in a mesh: dom: 64 (over z, core), sub: 16 (over y, x).
Axes of the slice: x: 4, y: 4, z: 32, core: 2. Of those that a mesh axis runs over, the one named last changes fastest.
Arguments:
- a_tiles: bfloat16 [4096, 10, 128, 128], P(('dom', 'sub')), may hold values from -0.5 to 0.5
- a_cols: int32 [4096, 10], P(('dom', 'sub')), may hold values from 0 to 4095, as said below
- a_count: int32 [4096], P(('dom', 'sub')), may hold values from 3 to 10, as said below
- p_tiles: bfloat16 [4096, 128, 256], P(('dom', 'sub')), may hold values from -0.5 to 0.5
- p_cols: int32 [4096, 2], P(('dom', 'sub')), may hold values from 0 to 511, as said below
Outputs:
- coarse_band: bfloat16 [65536, 3072], P(('dom', 'sub'))
The draws below stay inside these ranges and needn't reach their ends.
Inputs may be any that keep to these rules, and one draw needn't show every extreme that they name: `a_cols`: slot 0 of fine tile f holds f itself. Every column tile of fine tile f lies in its group g(f), or among the last 4 tiles of group g(f) - 1, or among the first 4 tiles of group g(f) + 1. Values in slots at or beyond a_count are such tiles too. `a_count`: each device has at least one fine row tile with all 10 slots live. `p_cols`: both coarse tiles of fine tile f lie in group g(f), between g(f) * 8 and (g(f) + 1) * 8 - 1. With j = f mod 64, the first, h, is within 1 of g(f) * 8 + (j * 8) // 64; the second is g(f) * 8 + (h - g(f) * 8 + 8 // 2) mod 8.
All inputs are finite; a program needn't handle non-finite values.
Results may differ from the reference program's by a relative error of at most 0.0049.
Values may be sent and summed in bfloat16 or wider, within the bound.
A program may use at most 128 MiB of HBM per device.

```python
import jax
import jax.numpy as jnp
from jax import lax

TILE = 128
ROW_TILES = 4
SLOTS = 10
GROUP_TILES = 64
COARSE_GROUP = 8
GROUPS = 64
FINE_TILES = 4096
COARSE_TILES = 512


def draw_a_cols(key, part):
    key = jax.random.fold_in(key, 7)
    key_region, key_own, key_edge = jax.random.split(key, 3)
    tile_ids = jnp.arange(FINE_TILES, dtype=jnp.int32)[:, None]
    group_ids = tile_ids // GROUP_TILES
    region = jax.random.randint(key_region, (FINE_TILES, SLOTS), 0, 10)
    own_tiles = group_ids * GROUP_TILES + jax.random.randint(key_own, (FINE_TILES, SLOTS), 0, GROUP_TILES)
    edge_offset = jax.random.randint(key_edge, (FINE_TILES, SLOTS), 0, ROW_TILES)
    left_tiles = group_ids * GROUP_TILES - ROW_TILES + edge_offset
    right_tiles = (group_ids + 1) * GROUP_TILES + edge_offset
    chosen = jnp.where((region == 0) & (group_ids > 0), left_tiles, jnp.where((region == 1) & (group_ids < GROUPS - 1), right_tiles, own_tiles))
    chosen = chosen.at[:, 0].set(tile_ids[:, 0])
    return chosen.astype(jnp.int32)


def draw_a_count(key, part):
    key = jax.random.fold_in(key, 11)
    key_count, key_full = jax.random.split(key)
    counts = jax.random.randint(key_count, (FINE_TILES,), 3, SLOTS + 1)
    full_rows = jax.random.randint(key_full, (FINE_TILES // ROW_TILES,), 0, ROW_TILES)
    tile_ids = jnp.arange(FINE_TILES, dtype=jnp.int32)
    counts = jnp.where(tile_ids % ROW_TILES == full_rows[tile_ids // ROW_TILES], SLOTS, counts)
    return counts.astype(jnp.int32)


def draw_p_cols(key, part):
    key = jax.random.fold_in(key, 5)
    key_jitter = jax.random.fold_in(key, 0)
    tile_ids = jnp.arange(FINE_TILES, dtype=jnp.int32)
    group_ids = tile_ids // GROUP_TILES
    local_ids = tile_ids % GROUP_TILES
    base_tile = local_ids * COARSE_GROUP // GROUP_TILES
    jitter = jax.random.randint(key_jitter, (FINE_TILES,), -1, 2)
    jitter = jnp.where((local_ids == 0) | (local_ids == GROUP_TILES - 1), 0, jitter)
    home_tile = jnp.clip(base_tile + jitter, 0, COARSE_GROUP - 1)
    other_tile = (home_tile + COARSE_GROUP // 2) % COARSE_GROUP
    both = jnp.stack([group_ids * COARSE_GROUP + home_tile, group_ids * COARSE_GROUP + other_tile], axis=1)
    return both.astype(jnp.int32)


def block_scale(stream_key, extent, cuts, least, largest):
    factor_of = 1.0
    for axis_at, blocks in cuts:
        heights = jax.random.uniform(jax.random.fold_in(jax.random.fold_in(stream_key, 6), axis_at), (blocks,), jnp.float32, least / len(cuts), largest / len(cuts))
        factor_of = factor_of * jnp.repeat(jnp.exp(heights), extent[axis_at] // blocks).reshape((-1,) + (1,) * (len(extent) - 1 - axis_at))
    return factor_of


def gaussian(rng, extent, scale, reach, shards=(), kind=jnp.bfloat16):
    loudness = block_scale(rng, extent, shards, -0.22, 0.18) if shards else 1.0
    entries = jax.random.normal(rng, extent, jnp.float32) * scale * loudness
    return jnp.minimum(jnp.maximum(entries, -reach), reach).astype(kind)


def setup_inputs(seed: int = 0) -> dict:
    key_of = jax.random.split(jax.random.key(seed), 6)
    a_tiles = gaussian(key_of[0], (FINE_TILES, SLOTS, TILE, TILE), TILE ** -0.5, 0.5, ((0, 1024),))
    a_cols = draw_a_cols(jax.random.fold_in(key_of[5], 71), 0)
    a_count = draw_a_count(jax.random.fold_in(key_of[5], 71), 0)
    p_tiles = gaussian(key_of[3], (FINE_TILES, TILE, 2 * TILE), TILE ** -0.5, 0.5, ((0, 1024),))
    p_cols = draw_p_cols(jax.random.fold_in(key_of[5], 71), 0)
    return dict(a_tiles=a_tiles, a_cols=a_cols, a_count=a_count, p_tiles=p_tiles, p_cols=p_cols)


def reference(a_tiles, a_cols, a_count, p_tiles, p_cols):
    slot_count = a_tiles.shape[1]
    tile_size = a_tiles.shape[2]
    block_ids = jnp.arange(slot_count, dtype=jnp.int32)
    band_blocks = 3 * COARSE_GROUP

    def tile_terms(a_row, column_ids, live_count, p_row, p_home, group_id):
        fetched = p_tiles[column_ids].astype(jnp.float32)
        products = jnp.einsum("kab,kbc->kac", a_row.astype(jnp.float32), fetched, precision=lax.Precision.HIGHEST)
        live_slots = (block_ids < live_count).astype(jnp.float32)
        products = products * live_slots[:, None, None]
        block_index = p_cols[column_ids] - (group_id - 1) * COARSE_GROUP
        pieces = products.reshape(slot_count, tile_size, 2, tile_size).transpose(0, 2, 1, 3)
        q_block = jnp.zeros((band_blocks, tile_size, tile_size), jnp.float32).at[block_index].add(pieces)
        q_block = q_block.transpose(1, 0, 2).reshape(tile_size, band_blocks * tile_size).astype(jnp.bfloat16)
        contribution = jnp.einsum("ab,ac->bc", p_row.astype(jnp.float32), q_block.astype(jnp.float32), precision=lax.Precision.HIGHEST)
        return contribution.reshape(2, tile_size, band_blocks * tile_size)

    def accumulate(coarse, block_start):
        tile_ids = block_start * ROW_TILES + jnp.arange(ROW_TILES, dtype=jnp.int32)
        group_ids = tile_ids // GROUP_TILES
        terms = jax.vmap(tile_terms)(a_tiles[tile_ids], a_cols[tile_ids], a_count[tile_ids], p_tiles[tile_ids], p_cols[tile_ids], group_ids)
        coarse = coarse.at[p_cols[tile_ids]].add(terms)
        return coarse, None

    start_coarse = jnp.zeros((COARSE_TILES, tile_size, band_blocks * tile_size), jnp.float32)
    coarse, _ = lax.scan(accumulate, start_coarse, jnp.arange(FINE_TILES // ROW_TILES, dtype=jnp.int32))
    return coarse.reshape(COARSE_TILES * tile_size, band_blocks * tile_size).astype(jnp.bfloat16)
```

```python
import jax
import jax.numpy as jnp
from jax import lax
from jax.experimental import pallas as pl
from jax.experimental.pallas import tpu as pltpu
from jax.sharding import PartitionSpec as P

MESH = pl.DeviceIdType.MESH

AXES = 4
CUBE = 16
LEFT, RIGHT = CUBE, CUBE + 1
GATHER = [(step, 0 if piece == 0 else 2 ** (piece - 1), 1 if piece == 0 else 2 ** (piece - 1))
          for step in range(AXES) for piece in range(step + 1)]
BASE = [0, 8, 12, 14]
REDUCE = [(step, BASE[step] + (0 if piece == 0 else 2 ** (piece - 1)), 1 if piece == 0 else 2 ** (piece - 1))
          for step in range(AXES) for piece in reversed(range(AXES - step))]


def cube_bits(x, y):
    return [(x + x // 2) % 2, (y + y // 2) % 2, x // 2, y // 2]


def rotated(rel, part):
    power = (1 + part % 2) * (1 + 3 * (part // 2))
    return rel // power + (rel % power) * (CUBE // power)


def kernel(a_hbm, cols, count, p_ref, pcols, out_ref, pool, meta, a_ref, prod, pair_of, q, pt, keep, sent, got,
           a_sem, ag_send, ag_recv, meta_send, meta_recv, halo_send, halo_recv, rs_send, rs_recv):
    f_tiles, slots, tile = a_ref.shape[0], a_ref.shape[1], a_ref.shape[2]
    unit = keep.shape[2]
    width = keep.shape[3]
    dom, sub = lax.axis_index("dom"), lax.axis_index("sub")
    doms = lax.axis_size("dom")
    x, y = lax.rem(sub, 4), lax.div(sub, 4)
    bits = cube_bits(x, y)
    xa, xb = x + 1 - 2 * (x % 2), 3 - x
    ya, yb = y + 1 - 2 * (y % 2), 3 - y

    def partner(axis):
        in_x, high = (axis + 1) % 2, axis // 2
        px = in_x * ((1 - high) * xa + high * xb) + (1 - in_x) * x
        py = (1 - in_x) * ((1 - high) * ya + high * yb) + in_x * y
        return (dom, py * 4 + px)

    after = (lax.rem(dom + 1, doms), sub)
    before = (lax.rem(dom + doms - 1, doms), sub)

    barrier = pltpu.get_barrier_semaphore()
    for other in [partner(axis) for axis in range(AXES)] + [after, before]:
        pl.semaphore_signal(barrier, inc=1, device_id=other, device_id_type=MESH)

    a_copy = pltpu.make_async_copy(a_hbm, a_ref, a_sem)
    a_copy.start()

    def arrange(i, carry):
        high = (pcols[i, 0] - dom * 8) // 4
        first = p_ref[i, :, :tile].astype(jnp.float32)
        second = p_ref[i, :, tile:].astype(jnp.float32)
        swap = jnp.full(first.shape, high, jnp.int32) != 0
        pool[i, 0, :, :tile] = jnp.where(swap, second, first).astype(jnp.bfloat16)
        pool[i, 0, :, tile:] = jnp.where(swap, first, second).astype(jnp.bfloat16)
        meta[0, i] = jnp.full(meta.shape[2:], pcols[i, 0] % 4, jnp.int32)
        return carry

    lax.fori_loop(0, f_tiles, arrange, 0)
    pl.semaphore_wait(barrier, 6)

    def gather_copy(i, at):
        step, first, number = GATHER[at]
        return pltpu.make_async_remote_copy(
            src_ref=pool.at[i, pl.ds(first, number)],
            dst_ref=pool.at[i, pl.ds(first + 2 ** step, number)],
            send_sem=ag_send.at[i, at],
            recv_sem=ag_recv.at[i, at],
            device_id=partner((i + step) % AXES),
            device_id_type=MESH,
        )

    def meta_copy(at):
        step, first, number = GATHER[at]
        return pltpu.make_async_remote_copy(
            src_ref=meta.at[pl.ds(first, number)],
            dst_ref=meta.at[pl.ds(first + 2 ** step, number)],
            send_sem=meta_send.at[at],
            recv_sem=meta_recv.at[at],
            device_id=partner(step),
            device_id_type=MESH,
        )

    for at, (step, first, number) in enumerate(GATHER):
        if first == 0:
            meta_copy(at).start()

            def send_own(i, carry, at=at):
                gather_copy(i, at).start()
                return carry

            lax.fori_loop(0, AXES, send_own, 0)

    for f in range(f_tiles):
        turned = pool[f, 0].astype(jnp.float32).T
        pair = jnp.full(turned.shape, pcols[f, 0] % 4, jnp.int32)
        for r in range(AXES):
            pt[r, :, f * tile:(f + 1) * tile] = jnp.where(pair == r, turned, 0.0).astype(jnp.bfloat16)

    for step in range(AXES):
        arrived = [at for at in range(len(GATHER)) if GATHER[at][0] == step]
        onward = [at for at in range(len(GATHER)) if GATHER[at][0] > step and GATHER[at][1] == 2 ** step]
        for at in arrived:
            meta_copy(at).wait_recv()
        for at in onward:
            meta_copy(at).start()

        def pass_on(i, carry, arrived=arrived, onward=onward):
            for at in arrived:
                gather_copy(i, at).wait_recv()
            for at in onward:
                gather_copy(i, at).start()
            return carry

        lax.fori_loop(0, AXES, pass_on, 0)

    def away(source):
        theirs = cube_bits(source % 4, source // 4)
        return sum(((bits[axis] + theirs[axis]) % 2) * 2 ** axis for axis in range(AXES))

    last, head = away(CUBE - 1), away(0)

    def halo_copy(i, side):
        rel, other = ((last, after), (head, before))[side]
        return pltpu.make_async_remote_copy(
            src_ref=pool.at[i, rotated(rel, i)],
            dst_ref=pool.at[i, CUBE + side],
            send_sem=halo_send.at[side, i],
            recv_sem=halo_recv.at[side, i],
            device_id=other,
            device_id_type=MESH,
        )

    def halo_meta(side):
        rel, other = ((last, after), (head, before))[side]
        return pltpu.make_async_remote_copy(
            src_ref=meta.at[rel],
            dst_ref=meta.at[CUBE + side],
            send_sem=halo_send.at[side, f_tiles],
            recv_sem=halo_recv.at[side, f_tiles],
            device_id=other,
            device_id_type=MESH,
        )

    for side in range(2):
        halo_meta(side).start()

    def halo_start(i, carry):
        for side in range(2):
            halo_copy(i, side).start()
        return carry

    lax.fori_loop(0, f_tiles, halo_start, 0)
    a_copy.wait()
    for side in range(2):
        halo_meta(side).wait_recv()

    def halo_wait(i, carry):
        for side in range(2):
            halo_copy(i, side).wait_recv()
        return carry

    lax.fori_loop(0, f_tiles, halo_wait, 0)

    def place(column):
        u = column - dom * (CUBE * f_tiles) + f_tiles
        part, at = u % f_tiles, u // f_tiles
        source = (at + CUBE - 1) % CUBE
        rel = away(source)
        turned = [rotated(rel, i) for i in range(AXES)]
        slot = jnp.where(part == 0, turned[0], jnp.where(part == 1, turned[1], jnp.where(part == 2, turned[2], turned[3])))
        is_left, is_right = at == 0, at == CUBE + 1
        slot = jnp.where(is_left, LEFT, jnp.where(is_right, RIGHT, slot))
        rel = jnp.where(is_left, LEFT, jnp.where(is_right, RIGHT, rel))
        offset = jnp.where(is_left, -2, jnp.where(is_right, 6, 2))
        return part, slot, rel, offset

    def multiply(f, carry):
        def one(k, carry):
            part, slot, rel, offset = place(cols[f, k])
            product = jnp.dot(a_ref[f, k], pool[part, slot], preferred_element_type=jnp.float32)
            for half in range(2):
                prod[f, k, half] = product[:, half * tile:(half + 1) * tile].reshape(prod.shape[3:])
            offset = jnp.where(k < count[f], offset, -100)
            pair_of[f, k] = meta[rel, part] + offset
            return carry

        return lax.fori_loop(0, slots, one, carry)

    lax.fori_loop(0, f_tiles, multiply, 0)

    def reduce_copy(i, at):
        step, first, number = REDUCE[at]
        return pltpu.make_async_remote_copy(
            src_ref=sent.at[i, pl.ds(first if step == 0 else first + 8, number)],
            dst_ref=got.at[i, pl.ds(first, number)],
            send_sem=rs_send.at[i, at],
            recv_sem=rs_recv.at[i, at],
            device_id=partner((i + AXES - 1 - step) % AXES),
            device_id_type=MESH,
        )

    def start_reduce(i, step):
        for at in range(len(REDUCE)):
            if REDUCE[at][0] == step:
                reduce_copy(i, at).start()

    def terms(i, carry):
        def add_up(f, carry):
            for j in range(2):
                for half in range(2):
                    total = jnp.zeros(prod.shape[3:], jnp.float32)
                    for k in range(slots):
                        live = (pair_of[f, k] == 2 * i + j).astype(jnp.float32)
                        total = total + prod[f, k, half] * live[None]
                    rows = pl.ds(pl.multiple_of(f * tile, tile), tile)
                    q[2 * i + j, rows, half * tile:(half + 1) * tile] = total.reshape(tile, tile).astype(jnp.bfloat16)
            return carry

        lax.fori_loop(0, f_tiles, add_up, 0)
        for j in range(2):
            columns = slice(j * 2 * tile, (j + 1) * 2 * tile)
            for r in range(AXES):
                block = jnp.dot(pt[r], q[2 * i + j], preferred_element_type=jnp.float32)
                for at in range(4):
                    upper, half = at // 2, at % 2
                    slot = rotated(away(2 * r + half + 8 * upper), i)
                    rows = block[upper * tile + half * unit:upper * tile + (half + 1) * unit]
                    keep[i, slot, :, columns] = rows
                    sent[i, (slot + 8) % CUBE, :, columns] = rows.astype(jnp.bfloat16)
        start_reduce(i, 0)
        return carry

    lax.fori_loop(0, AXES, terms, 0)

    def total_of(i, low, step):
        number = max(low, 1)
        for at, (earlier, first, _) in enumerate(REDUCE):
            if earlier < step and first == BASE[earlier] + low:
                reduce_copy(i, at).wait_recv()
        value = keep[i, low:low + number]
        for earlier in range(step):
            value = value + got[i, BASE[earlier] + low:BASE[earlier] + low + number].astype(jnp.float32)
        return value.astype(jnp.bfloat16)

    for step in range(1, AXES):
        low = 2 ** (AXES - 1 - step)

        def send_on(i, carry, step=step, low=low):
            sent[i, BASE[step] + 8:BASE[step] + 8 + low] = total_of(i, low, step)
            start_reduce(i, step)
            return carry

        lax.fori_loop(0, AXES, send_on, 0)

    empty = jnp.zeros((unit, 2 * tile), jnp.bfloat16)
    for block in (0, 4, 18, 22):
        out_ref[:, block * tile:(block + 2) * tile] = empty
    for i in range(AXES):
        mine = total_of(i, 0, AXES)[0]
        for j in range(2):
            pair = 2 * i + j
            block = pair + 2 if pair < 2 else (pair + 6 if pair < 6 else pair + 10)
            for half in range(2):
                columns = slice((block + 4 * half) * tile, (block + 4 * half + 1) * tile)
                out_ref[:, columns] = mine[:, (2 * j + half) * tile:(2 * j + half + 1) * tile]

    def sent_off(i, carry):
        for at in range(len(GATHER)):
            gather_copy(i, at).wait_send()
        for at in range(len(REDUCE)):
            reduce_copy(i, at).wait_send()
        for side in range(2):
            halo_copy(i, side).wait_send()
        return carry

    lax.fori_loop(0, AXES, sent_off, 0)
    for at in range(len(GATHER)):
        meta_copy(at).wait_send()
    for side in range(2):
        halo_meta(side).wait_send()


def local(a_tiles, a_cols, a_count, p_tiles, p_cols):
    f_tiles, slots, tile, _ = a_tiles.shape
    unit = 64
    vmem, smem = pl.BlockSpec(memory_space=pltpu.VMEM), pl.BlockSpec(memory_space=pltpu.SMEM)
    dma = pltpu.SemaphoreType.DMA
    return pl.pallas_call(
        kernel,
        out_shape=jax.ShapeDtypeStruct((unit, 24 * tile), jnp.bfloat16),
        in_specs=[pl.BlockSpec(memory_space=pl.ANY), smem, smem, vmem, smem],
        out_specs=vmem,
        scratch_shapes=[
            pltpu.VMEM((f_tiles, CUBE + 2, tile, 2 * tile), jnp.bfloat16),
            pltpu.VMEM((CUBE + 2, f_tiles, 8, tile), jnp.int32),
            pltpu.VMEM((f_tiles, slots, tile, tile), jnp.bfloat16),
            pltpu.VMEM((f_tiles, slots, 2, tile // 8, 8, tile), jnp.float32),
            pltpu.VMEM((f_tiles, slots, 8, tile), jnp.int32),
            pltpu.VMEM((8, f_tiles * tile, 2 * tile), jnp.bfloat16),
            pltpu.VMEM((AXES, 2 * tile, f_tiles * tile), jnp.bfloat16),
            pltpu.VMEM((AXES, CUBE, unit, 4 * tile), jnp.float32),
            pltpu.VMEM((AXES, CUBE + 7, unit, 4 * tile), jnp.bfloat16),
            pltpu.VMEM((AXES, 15, unit, 4 * tile), jnp.bfloat16),
            dma,
            dma((AXES, len(GATHER))),
            dma((AXES, len(GATHER))),
            dma((len(GATHER),)),
            dma((len(GATHER),)),
            dma((2, f_tiles + 1)),
            dma((2, f_tiles + 1)),
            dma((AXES, len(REDUCE))),
            dma((AXES, len(REDUCE))),
        ],
        compiler_params=pltpu.CompilerParams(collective_id=0, has_side_effects=True, vmem_limit_bytes=48 * 2 ** 20),
    )(a_tiles, a_cols, a_count, p_tiles, p_cols)


def solution(mesh):
    placed = (
        P(("dom", "sub"), None, None, None),
        P(("dom", "sub"), None),
        P(("dom", "sub")),
        P(("dom", "sub"), None, None),
        P(("dom", "sub"), None),
    )
    return jax.shard_map(
        local, mesh=mesh, in_specs=placed, out_specs=P(("dom", "sub"), None), check_vma=False
    )
```

```python
import jax
import jax.numpy as jnp
from jax import lax
from jax.experimental import pallas as pl
from jax.experimental.pallas import tpu as pltpu
from jax.sharding import PartitionSpec as P

MESH = pl.DeviceIdType.MESH

AXES = 4
CUBE = 16
LEFT, RIGHT = CUBE, CUBE + 1
GATHER = [(0, 0), (0, 1), (0, 2), (1, 1), (0, 3), (1, 2), (2, 2), (3, 2), (1, 3), (2, 3), (3, 3),
          (4, 3), (5, 3), (6, 3), (7, 3)]
GATHER_DEPTH = 3
BASE = [0, 8, 12, 14]
REDUCE = [(0, 6, 2), (0, 4, 2), (1, 10, 2), (0, 2, 2), (1, 9, 1), (0, 1, 1), (2, 13, 1), (1, 8, 1), (0, 0, 1),
          (2, 12, 1), (3, 14, 1)]
REDUCE_DEPTH = 2


def cube_bits(x, y):
    return [(x + x // 2) % 2, (y + y // 2) % 2, x // 2, y // 2]


def rotated(rel, part):
    power = (1 + part % 2) * (1 + 3 * (part // 2))
    return rel // power + (rel % power) * (CUBE // power)


def kernel(a_hbm, cols, count, p_hbm, pcols, out_ref, pool, meta, a_ref, p_ref, turned, pt, prod, q, keep, leaf, sent, got,
           meta_s, where_s, prev_s, last_s,
           a_sem, p_sem, s_sem, ag_send, ag_recv, meta_send, meta_recv, halo_send, halo_recv, rs_send, rs_recv):
    f_tiles, slots, tile = a_ref.shape[0], a_ref.shape[1], a_ref.shape[2]
    unit = keep.shape[2]
    dom, sub = lax.axis_index("dom"), lax.axis_index("sub")
    doms = lax.axis_size("dom")
    x, y = sub % 4, sub // 4
    bits = cube_bits(x, y)
    xa, xb = x + 1 - 2 * (x % 2), 3 - x
    ya, yb = y + 1 - 2 * (y % 2), 3 - y

    def partner(axis):
        in_x, high = (axis + 1) % 2, axis // 2
        px = in_x * ((1 - high) * xa + high * xb) + (1 - in_x) * x
        py = (1 - in_x) * ((1 - high) * ya + high * yb) + in_x * y
        return (dom, py * 4 + px)

    def away(source):
        theirs = cube_bits(source % 4, source // 4)
        return sum(((bits[axis] + theirs[axis]) % 2) * 2 ** axis for axis in range(AXES))

    after = (lax.rem(dom + 1, doms), sub)
    before = (lax.rem(dom + doms - 1, doms), sub)

    p_copy = pltpu.make_async_copy(p_hbm, p_ref, p_sem)
    p_copy.start()
    barrier = pltpu.get_barrier_semaphore()
    for other in [partner(axis) for axis in range(AXES)] + [after, before]:
        pl.semaphore_signal(barrier, inc=1, device_id=other, device_id_type=MESH)
    a_copy = pltpu.make_async_copy(a_hbm, a_ref, a_sem)
    a_copy.start()

    lanes = lax.broadcasted_iota(jnp.int32, meta.shape[1:], 1)
    meta[0] = sum(jnp.where(lanes == f, pcols[0, f] % 4, 0) for f in range(f_tiles))
    p_copy.wait()

    def arrange(i, carry):
        high = (pcols[0, i] - dom * 8) // 4
        first = p_ref[i, :, :tile].astype(jnp.float32)
        second = p_ref[i, :, tile:].astype(jnp.float32)
        swap = jnp.full(first.shape, high, jnp.int32) != 0
        pool[i, 0, :, :tile] = jnp.where(swap, second, first).astype(jnp.bfloat16)
        pool[i, 0, :, tile:] = jnp.where(swap, first, second).astype(jnp.bfloat16)
        return carry

    lax.fori_loop(0, f_tiles, arrange, 0)
    pl.semaphore_wait(barrier, 6)

    last, head = away(CUBE - 1), away(0)

    def final_slot(i, at):
        ahead, behind = rotated(last, i), rotated(head, i)
        begin = jnp.where(ahead // 4 == 1, ahead % 4, jnp.where(behind // 4 == 1, behind % 4, 0))
        return 4 + (at - (len(GATHER) - 4) + begin) % 4

    def gather_copy(i, at):
        slot, step = GATHER[at]
        if slot >= 4:
            slot = final_slot(i, at)
        landing = slot + 2 ** step
        return pltpu.make_async_remote_copy(
            src_ref=pool.at[i, slot],
            dst_ref=pool.at[i, landing],
            send_sem=ag_send.at[i, at],
            recv_sem=ag_recv.at[i, landing],
            device_id=partner((i + step) % AXES),
            device_id_type=MESH,
        )

    def arrival(i, slot):
        return pltpu.make_async_copy(pool.at[i, slot], pool.at[i, slot], ag_recv.at[i, slot])

    def meta_copy(step):
        return pltpu.make_async_remote_copy(
            src_ref=meta.at[pl.ds(0, 2 ** step)],
            dst_ref=meta.at[pl.ds(2 ** step, 2 ** step)],
            send_sem=meta_send.at[step],
            recv_sem=meta_recv.at[step],
            device_id=partner(step),
            device_id_type=MESH,
        )

    def halo_copy(i, side):
        rel, other = ((last, after), (head, before))[side]
        return pltpu.make_async_remote_copy(
            src_ref=pool.at[i, rotated(rel, i)],
            dst_ref=pool.at[i, CUBE + side],
            send_sem=halo_send.at[side, i],
            recv_sem=halo_recv.at[side, i],
            device_id=other,
            device_id_type=MESH,
        )

    def halo_meta(side):
        rel, other = ((last, after), (head, before))[side]
        return pltpu.make_async_remote_copy(
            src_ref=meta.at[rel],
            dst_ref=meta.at[CUBE + side],
            send_sem=halo_send.at[side, f_tiles],
            recv_sem=halo_recv.at[side, f_tiles],
            device_id=other,
            device_id_type=MESH,
        )

    def place(f, carry):
        for k in range(slots):
            u = cols[f, k] - dom * (CUBE * f_tiles) + f_tiles
            part, at = u % f_tiles, u // f_tiles
            rel = away((at + CUBE - 1) % CUBE)
            turns = [rotated(rel, i) for i in range(AXES)]
            slot = jnp.where(part == 0, turns[0], jnp.where(part == 1, turns[1], jnp.where(part == 2, turns[2], turns[3])))
            is_left, is_right = at == 0, at == CUBE + 1
            where_s[0, f * slots + k] = part
            where_s[1, f * slots + k] = jnp.where(is_left, LEFT, jnp.where(is_right, RIGHT, slot))
            where_s[2, f * slots + k] = jnp.where(is_left, LEFT, jnp.where(is_right, RIGHT, rel))
            where_s[3, f * slots + k] = jnp.where(is_left, -2, jnp.where(is_right, 6, 2))
        return carry

    def turn(f, carry):
        turned[f] = pool[f, 0].astype(jnp.float32).T
        return carry

    def lay_out(i, carry):
        for f in range(f_tiles):
            pair = jnp.full((unit, tile), pcols[0, f] % 4, jnp.int32)
            for owner in range(CUBE):
                rows = slice((owner // 8) * tile + (owner % 2) * unit, (owner // 8) * tile + (owner % 2 + 1) * unit)
                slot = rotated(away(owner), i)
                value = jnp.where(pair == (owner // 2) % 4, turned[f, rows], 0.0).astype(jnp.bfloat16)
                pt[i, slot, :, f * tile:(f + 1) * tile] = value
        return carry

    def chain(f, carry):
        pairs = []
        for k in range(slots):
            at = f * slots + k
            pair = meta_s[where_s[2, at], 0, where_s[0, at]] + where_s[3, at]
            pairs.append(jnp.where(k < count[f], pair, -1))
        for k in range(slots):
            found = slots
            for earlier in range(k):
                found = jnp.where(pairs[earlier] == pairs[k], earlier, found)
            prev_s[f * slots + k] = jnp.int32(found)
        for pair in range(8):
            found = slots
            for k in range(slots):
                found = jnp.where(pairs[k] == pair, k, found)
            last_s[f * 8 + pair] = found
        return carry

    meta_copy(0).start()
    seen = {0}
    for at, (slot, step) in enumerate(GATHER):
        new = slot if slot not in seen else None
        seen.add(slot)

        def send(i, carry, at=at, new=new):
            if new is not None:
                arrival(i, new).wait()
            if at >= GATHER_DEPTH:
                gather_copy(i, at - GATHER_DEPTH).wait_send()
            gather_copy(i, at).start()
            return carry

        if slot == 4:
            def early(i, carry):
                for late in range(4, 8):
                    arrival(i, late).wait()
                for side, rel in enumerate((last, head)):
                    @pl.when(rotated(rel, i) < 8)
                    def _():
                        halo_copy(i, side).start()
                return carry

            seen.update(range(4, 8))
            lax.fori_loop(0, AXES, early, 0)

            def send(i, carry, at=at):
                gather_copy(i, at - GATHER_DEPTH).wait_send()
                gather_copy(i, at).start()
                return carry

        lax.fori_loop(0, AXES, send, 0)
        if at == 1:
            lax.fori_loop(0, f_tiles, turn, 0)
        if at == 2:
            lax.fori_loop(0, 2, lay_out, 0)
        if at == 3:
            meta_copy(0).wait_recv()
            meta_copy(1).start()
        if at == 4:
            lax.fori_loop(2, AXES, lay_out, 0)
        if at == 5:
            meta_copy(1).wait_recv()
            meta_copy(2).start()
        if at == 6:
            lax.fori_loop(0, f_tiles, place, 0)
        if at == 8:
            meta_copy(2).wait_recv()
            meta_copy(3).start()
        if at == 11:
            meta_copy(3).wait_recv()
            for side in range(2):
                halo_meta(side).start()
        if at == 13:
            for side in range(2):
                halo_meta(side).wait_recv()
            to_scalars = pltpu.make_async_copy(meta, meta_s, s_sem)
            to_scalars.start()
            to_scalars.wait()
            lax.fori_loop(0, f_tiles, chain, 0)

    for f in range(f_tiles):
        prod[f, slots] = jnp.zeros(prod.shape[2:], jnp.float32)

    def late(i, carry):
        for side, rel in enumerate((last, head)):
            mine = rotated(rel, i)

            @pl.when(mine >= 8)
            def _():
                arrival(i, mine).wait()
                halo_copy(i, side).start()
        return carry

    lax.fori_loop(0, AXES, late, 0)

    def rest(i, carry):
        ahead, behind = rotated(last, i), rotated(head, i)
        for slot in range(8, CUBE):
            @pl.when((slot - ahead) * (slot - behind) != 0)
            def _():
                arrival(i, slot).wait()
        return carry

    lax.fori_loop(0, AXES, rest, 0)
    a_copy.wait()

    def halo_wait(i, carry):
        for side in range(2):
            halo_copy(i, side).wait_recv()
        return carry

    lax.fori_loop(0, f_tiles, halo_wait, 0)

    def multiply(f, carry):
        for k in range(slots):
            at = f * slots + k
            product = jnp.dot(a_ref[f, k], pool[where_s[0, at], where_s[1, at]], preferred_element_type=jnp.float32)
            prod[f, k] = product + prod[f, prev_s[at]] if k else product
        return carry

    lax.fori_loop(0, f_tiles, multiply, 0)

    def reduce_copy(i, at):
        step, first, number = REDUCE[at]
        return pltpu.make_async_remote_copy(
            src_ref=leaf.at[i, pl.ds(first, number)] if step == 0 else sent.at[i, pl.ds(first - 8, number)],
            dst_ref=got.at[i, pl.ds(first, number)],
            send_sem=rs_send.at[i, at],
            recv_sem=rs_recv.at[i, at],
            device_id=partner((i + AXES - 1 - step) % AXES),
            device_id_type=MESH,
        )

    def far_terms(i, carry):
        for j in range(2):
            for f in range(f_tiles):
                rows = slice(f * tile, (f + 1) * tile)
                q[2 * i + j, rows] = prod[f, last_s[f * 8 + 2 * i + j]].astype(jnp.bfloat16)
        far = pt[i, 8:].reshape(8 * unit, f_tiles * tile)
        for j in range(2):
            columns = slice(j * 2 * tile, (j + 1) * 2 * tile)
            block = jnp.dot(far, q[2 * i + j], preferred_element_type=jnp.float32)
            leaf[i, :, :, columns] = block.reshape(8, unit, 2 * tile).astype(jnp.bfloat16)
        for at in range(REDUCE_DEPTH):
            reduce_copy(i, at).start()
        return carry

    lax.fori_loop(0, AXES, far_terms, 0)

    def near_terms(i, carry):
        near = pt[i, :8].reshape(8 * unit, f_tiles * tile)
        for j in range(2):
            columns = slice(j * 2 * tile, (j + 1) * 2 * tile)
            block = jnp.dot(near, q[2 * i + j], preferred_element_type=jnp.float32)
            keep[i, :, :, columns] = block.reshape(8, unit, 2 * tile)
        return carry

    lax.fori_loop(0, AXES, near_terms, 0)

    taken = set()

    def waits(step, low, number):
        found = []
        for at, (earlier, first, length) in enumerate(REDUCE):
            begin = first - BASE[earlier]
            if earlier < step and begin < low + number and low < begin + length and at not in taken:
                taken.add(at)
                found.append(at)
        return found

    def total_of(i, step, low, number):
        value = keep[i, low:low + number]
        for earlier in range(step):
            value = value + got[i, BASE[earlier] + low:BASE[earlier] + low + number].astype(jnp.float32)
        return value.astype(jnp.bfloat16)

    for at, (step, first, number) in enumerate(REDUCE):
        if at < REDUCE_DEPTH:
            continue
        low = 2 ** (AXES - 1 - step) + first - BASE[step]
        needed = waits(step, low, number) if step else []

        def send_on(i, carry, at=at, step=step, first=first, number=number, low=low, needed=needed):
            for other in needed:
                reduce_copy(i, other).wait_recv()
            if step:
                sent[i, first - 8:first - 8 + number] = total_of(i, step, low, number)
            reduce_copy(i, at - REDUCE_DEPTH).wait_send()
            reduce_copy(i, at).start()
            return carry

        lax.fori_loop(0, AXES, send_on, 0)

    empty = jnp.zeros((unit, 2 * tile), jnp.bfloat16)
    for block in (0, 4, 18, 22):
        out_ref[:, block * tile:(block + 2) * tile] = empty
    needed = waits(AXES, 0, 1)
    for i in range(AXES):
        for other in needed:
            reduce_copy(i, other).wait_recv()
        mine = total_of(i, AXES, 0, 1)[0]
        for j in range(2):
            pair = 2 * i + j
            block = pair + 2 if pair < 2 else (pair + 6 if pair < 6 else pair + 10)
            for half in range(2):
                columns = slice((block + 4 * half) * tile, (block + 4 * half + 1) * tile)
                out_ref[:, columns] = mine[:, (2 * j + half) * tile:(2 * j + half + 1) * tile]

    def sent_off(i, carry):
        for at in range(len(GATHER) - GATHER_DEPTH, len(GATHER)):
            gather_copy(i, at).wait_send()
        for at in range(len(REDUCE) - REDUCE_DEPTH, len(REDUCE)):
            reduce_copy(i, at).wait_send()
        for side in range(2):
            halo_copy(i, side).wait_send()
        return carry

    lax.fori_loop(0, AXES, sent_off, 0)
    for step in range(AXES):
        meta_copy(step).wait_send()
    for side in range(2):
        halo_meta(side).wait_send()


def local(a_tiles, a_cols, a_count, p_tiles, p_cols):
    f_tiles, slots, tile, _ = a_tiles.shape
    unit = 64
    hbm, smem = pl.BlockSpec(memory_space=pl.ANY), pl.BlockSpec(memory_space=pltpu.SMEM)
    dma = pltpu.SemaphoreType.DMA
    return pl.pallas_call(
        kernel,
        out_shape=jax.ShapeDtypeStruct((unit, 24 * tile), jnp.bfloat16),
        in_specs=[hbm, smem, smem, hbm, smem],
        out_specs=pl.BlockSpec(memory_space=pltpu.VMEM),
        scratch_shapes=[
            pltpu.VMEM((f_tiles, CUBE + 2, tile, 2 * tile), jnp.bfloat16),
            pltpu.VMEM((CUBE + 2, 8, tile), jnp.int32),
            pltpu.VMEM((f_tiles, slots, tile, tile), jnp.bfloat16),
            pltpu.VMEM((f_tiles, tile, 2 * tile), jnp.bfloat16),
            pltpu.VMEM((f_tiles, 2 * tile, tile), jnp.float32),
            pltpu.VMEM((AXES, CUBE, unit, f_tiles * tile), jnp.bfloat16),
            pltpu.VMEM((f_tiles, slots + 1, tile, 2 * tile), jnp.float32),
            pltpu.VMEM((8, f_tiles * tile, 2 * tile), jnp.bfloat16),
            pltpu.VMEM((AXES, 8, unit, 4 * tile), jnp.float32),
            pltpu.VMEM((AXES, 8, unit, 4 * tile), jnp.bfloat16),
            pltpu.VMEM((AXES, 7, unit, 4 * tile), jnp.bfloat16),
            pltpu.VMEM((AXES, 15, unit, 4 * tile), jnp.bfloat16),
            pltpu.SMEM((CUBE + 2, 8, tile), jnp.int32),
            pltpu.SMEM((4, f_tiles * slots), jnp.int32),
            pltpu.SMEM((f_tiles * slots,), jnp.int32),
            pltpu.SMEM((f_tiles * 8,), jnp.int32),
            dma,
            dma,
            dma,
            dma((AXES, len(GATHER))),
            dma((AXES, CUBE)),
            dma((AXES,)),
            dma((AXES,)),
            dma((2, f_tiles + 1)),
            dma((2, f_tiles + 1)),
            dma((AXES, len(REDUCE))),
            dma((AXES, len(REDUCE))),
        ],
        compiler_params=pltpu.CompilerParams(collective_id=0, has_side_effects=True, vmem_limit_bytes=60 * 2 ** 20),
    )(a_tiles, a_cols, a_count, p_tiles, p_cols.T)


def solution(mesh):
    placed = (
        P(("dom", "sub"), None, None, None),
        P(("dom", "sub"), None),
        P(("dom", "sub")),
        P(("dom", "sub"), None, None),
        P(("dom", "sub"), None),
    )
    return jax.shard_map(
        local, mesh=mesh, in_specs=placed, out_specs=P(("dom", "sub"), None), check_vma=False
    )
```

```python
import jax
import jax.numpy as jnp
from jax import lax
from jax.experimental import pallas as pl
from jax.experimental.pallas import tpu as pltpu
from jax.sharding import PartitionSpec as P

MESH = pl.DeviceIdType.MESH

AXES = 4
CUBE = 16
LEFT, RIGHT = CUBE, CUBE + 1
GATHER = [(0, 0), (0, 1), (0, 2), (1, 1), (0, 3), (1, 2), (2, 2), (3, 2), (1, 3), (2, 3), (3, 3),
          (4, 3), (5, 3), (6, 3), (7, 3)]
GATHER_DEPTH = 3
BASE = [0, 8, 12, 14]
REDUCE = [(0, 6, 2), (0, 4, 2), (1, 10, 2), (0, 2, 2), (1, 9, 1), (0, 1, 1), (2, 13, 1), (1, 8, 1), (0, 0, 1),
          (2, 12, 1), (3, 14, 1)]
REDUCE_DEPTH = 2


def cube_bits(x, y):
    return [(x + x // 2) % 2, (y + y // 2) % 2, x // 2, y // 2]


def rotated(rel, part):
    power = (1 + part % 2) * (1 + 3 * (part // 2))
    return rel // power + (rel % power) * (CUBE // power)


def kernel(a_hbm, cols, count, p_hbm, pcols, out_ref, pool, meta, a_ref, p_ref, turned, pt, prod, q, keep, leaf, sent, got,
           meta_s, where_s, prev_s, last_s,
           a_sem, p_sem, s_sem, ag_send, ag_recv, meta_send, meta_recv, halo_send, halo_recv, rs_send, rs_recv):
    f_tiles, slots, tile = a_ref.shape[0], a_ref.shape[1], a_ref.shape[2]
    unit = keep.shape[2]
    dom, sub = lax.axis_index("dom"), lax.axis_index("sub")
    doms = lax.axis_size("dom")
    x, y = sub % 4, sub // 4
    bits = cube_bits(x, y)
    xa, xb = x + 1 - 2 * (x % 2), 3 - x
    ya, yb = y + 1 - 2 * (y % 2), 3 - y

    def partner(axis):
        in_x, high = (axis + 1) % 2, axis // 2
        px = in_x * ((1 - high) * xa + high * xb) + (1 - in_x) * x
        py = (1 - in_x) * ((1 - high) * ya + high * yb) + in_x * y
        return (dom, py * 4 + px)

    def away(source):
        theirs = cube_bits(source % 4, source // 4)
        return sum(((bits[axis] + theirs[axis]) % 2) * 2 ** axis for axis in range(AXES))

    after = (lax.rem(dom + 1, doms), sub)
    before = (lax.rem(dom + doms - 1, doms), sub)

    p_copy = pltpu.make_async_copy(p_hbm, p_ref, p_sem)
    p_copy.start()
    barrier = pltpu.get_barrier_semaphore()
    for other in [partner(axis) for axis in range(AXES)] + [after, before]:
        pl.semaphore_signal(barrier, inc=1, device_id=other, device_id_type=MESH)
    a_copy = pltpu.make_async_copy(a_hbm, a_ref, a_sem)
    a_copy.start()

    lanes = lax.broadcasted_iota(jnp.int32, meta.shape[1:], 1)
    meta[0] = sum(jnp.where(lanes == f, pcols[0, f] % 4, 0) for f in range(f_tiles))
    p_copy.wait()

    def arrange(i, carry):
        high = (pcols[0, i] - dom * 8) // 4
        first = p_ref[i, :, :tile].astype(jnp.float32)
        second = p_ref[i, :, tile:].astype(jnp.float32)
        swap = jnp.full(first.shape, high, jnp.int32) != 0
        pool[i, 0, :, :tile] = jnp.where(swap, second, first).astype(jnp.bfloat16)
        pool[i, 0, :, tile:] = jnp.where(swap, first, second).astype(jnp.bfloat16)
        return carry

    lax.fori_loop(0, f_tiles, arrange, 0)
    pl.semaphore_wait(barrier, 6)

    last, head = away(CUBE - 1), away(0)

    def final_slot(i, at):
        ahead, behind = rotated(last, i), rotated(head, i)
        begin = jnp.where(ahead // 4 == 1, ahead % 4, jnp.where(behind // 4 == 1, behind % 4, 0))
        return 4 + (at - (len(GATHER) - 4) + begin) % 4

    def gather_copy(i, at):
        slot, step = GATHER[at]
        if slot >= 4:
            slot = final_slot(i, at)
        landing = slot + 2 ** step
        return pltpu.make_async_remote_copy(
            src_ref=pool.at[i, slot],
            dst_ref=pool.at[i, landing],
            send_sem=ag_send.at[i, at % GATHER_DEPTH],
            recv_sem=ag_recv.at[i, landing],
            device_id=partner((i + step) % AXES),
            device_id_type=MESH,
        )

    def arrival(i, slot):
        return pltpu.make_async_copy(pool.at[i, slot], pool.at[i, slot], ag_recv.at[i, slot])

    def meta_copy(step):
        return pltpu.make_async_remote_copy(
            src_ref=meta.at[pl.ds(0, 2 ** step)],
            dst_ref=meta.at[pl.ds(2 ** step, 2 ** step)],
            send_sem=meta_send.at[step],
            recv_sem=meta_recv.at[step],
            device_id=partner(step),
            device_id_type=MESH,
        )

    def halo_copy(i, side):
        rel, other = ((last, after), (head, before))[side]
        return pltpu.make_async_remote_copy(
            src_ref=pool.at[i, rotated(rel, i)],
            dst_ref=pool.at[i, CUBE + side],
            send_sem=halo_send.at[0, side],
            recv_sem=halo_recv.at[0, side],
            device_id=other,
            device_id_type=MESH,
        )

    def halo_meta(side):
        rel, other = ((last, after), (head, before))[side]
        return pltpu.make_async_remote_copy(
            src_ref=meta.at[rel],
            dst_ref=meta.at[CUBE + side],
            send_sem=halo_send.at[1, side],
            recv_sem=halo_recv.at[1, side],
            device_id=other,
            device_id_type=MESH,
        )

    def halo_all(side, sems):
        landed = pool.at[:, CUBE + side]
        return pltpu.make_async_copy(landed, landed, sems.at[0, side])

    def place(f, carry):
        for k in range(slots):
            u = cols[f, k] - dom * (CUBE * f_tiles) + f_tiles
            part, at = u % f_tiles, u // f_tiles
            rel = away((at + CUBE - 1) % CUBE)
            turns = [rotated(rel, i) for i in range(AXES)]
            slot = jnp.where(part == 0, turns[0], jnp.where(part == 1, turns[1], jnp.where(part == 2, turns[2], turns[3])))
            is_left, is_right = at == 0, at == CUBE + 1
            where_s[0, f * slots + k] = part
            where_s[1, f * slots + k] = jnp.where(is_left, LEFT, jnp.where(is_right, RIGHT, slot))
            where_s[2, f * slots + k] = jnp.where(is_left, LEFT, jnp.where(is_right, RIGHT, rel))
            where_s[3, f * slots + k] = jnp.where(is_left, -2, jnp.where(is_right, 6, 2))
        return carry

    def turn(f, carry):
        turned[f] = pool[f, 0].astype(jnp.float32).T
        return carry

    def lay_out(i, carry):
        for f in range(f_tiles):
            pair = jnp.full((unit, tile), pcols[0, f] % 4, jnp.int32)
            for owner in range(CUBE):
                rows = slice((owner // 8) * tile + (owner % 2) * unit, (owner // 8) * tile + (owner % 2 + 1) * unit)
                slot = rotated(away(owner), i)
                value = jnp.where(pair == (owner // 2) % 4, turned[f, rows], 0.0).astype(jnp.bfloat16)
                pt[i, slot, :, f * tile:(f + 1) * tile] = value
        return carry

    def chain(f, carry):
        pairs = []
        for k in range(slots):
            at = f * slots + k
            pair = meta_s[where_s[2, at], 0, where_s[0, at]] + where_s[3, at]
            pairs.append(jnp.where(k < count[f], pair, -1))
        for k in range(slots):
            found = slots
            for earlier in range(k):
                found = jnp.where(pairs[earlier] == pairs[k], earlier, found)
            prev_s[f * slots + k] = jnp.int32(found)
        for pair in range(8):
            found = slots
            for k in range(slots):
                found = jnp.where(pairs[k] == pair, k, found)
            last_s[f * 8 + pair] = found
        return carry

    meta_copy(0).start()
    seen = {0}
    for at, (slot, step) in enumerate(GATHER):
        new = slot if slot not in seen else None
        seen.add(slot)

        def send(i, carry, at=at, new=new):
            if new is not None:
                arrival(i, new).wait()
            if at >= GATHER_DEPTH:
                gather_copy(i, at - GATHER_DEPTH).wait_send()
            gather_copy(i, at).start()
            return carry

        if slot == 4:
            def early(i, carry):
                for late in range(4, 8):
                    arrival(i, late).wait()
                for side, rel in enumerate((last, head)):
                    @pl.when(rotated(rel, i) < 8)
                    def _():
                        halo_copy(i, side).start()
                return carry

            seen.update(range(4, 8))
            lax.fori_loop(0, AXES, early, 0)

            def send(i, carry, at=at):
                gather_copy(i, at - GATHER_DEPTH).wait_send()
                gather_copy(i, at).start()
                return carry

        lax.fori_loop(0, AXES, send, 0)
        if at == 1:
            lax.fori_loop(0, f_tiles, turn, 0)
        if at == 2:
            lax.fori_loop(0, 2, lay_out, 0)
        if at == 3:
            meta_copy(0).wait_recv()
            meta_copy(1).start()
        if at == 4:
            lax.fori_loop(2, AXES, lay_out, 0)
        if at == 5:
            meta_copy(1).wait_recv()
            meta_copy(2).start()
        if at == 8:
            meta_copy(2).wait_recv()
            meta_copy(3).start()
        if at == 11:
            meta_copy(3).wait_recv()
            for side in range(2):
                halo_meta(side).start()
        if at == 13:
            for side in range(2):
                halo_meta(side).wait_recv()
            to_scalars = pltpu.make_async_copy(meta, meta_s, s_sem)
            to_scalars.start()

    lax.fori_loop(0, f_tiles, place, 0)
    to_scalars.wait()
    lax.fori_loop(0, f_tiles, chain, 0)
    for f in range(f_tiles):
        prod[f, slots] = jnp.zeros(prod.shape[2:], jnp.float32)

    def late(i, carry):
        for side, rel in enumerate((last, head)):
            mine = rotated(rel, i)

            @pl.when(mine >= 8)
            def _():
                arrival(i, mine).wait()
                halo_copy(i, side).start()
        return carry

    lax.fori_loop(0, AXES, late, 0)

    def rest(i, carry):
        ahead, behind = rotated(last, i), rotated(head, i)
        for slot in range(8, CUBE):
            @pl.when((slot - ahead) * (slot - behind) != 0)
            def _():
                arrival(i, slot).wait()
        return carry

    lax.fori_loop(0, AXES, rest, 0)
    a_copy.wait()

    for side in range(2):
        halo_all(side, halo_recv).wait()

    def multiply(f, carry):
        for k in range(slots):
            at = f * slots + k
            product = jnp.dot(a_ref[f, k], pool[where_s[0, at], where_s[1, at]], preferred_element_type=jnp.float32)
            prod[f, k] = product + prod[f, prev_s[at]] if k else product
        return carry

    lax.fori_loop(0, f_tiles, multiply, 0)

    def reduce_copy(i, at):
        step, first, number = REDUCE[at]
        return pltpu.make_async_remote_copy(
            src_ref=leaf.at[i, pl.ds(first, number)] if step == 0 else sent.at[i, pl.ds(first - 8, number)],
            dst_ref=got.at[i, pl.ds(first, number)],
            send_sem=rs_send.at[i, at % REDUCE_DEPTH],
            recv_sem=rs_recv.at[i, at],
            device_id=partner((i + AXES - 1 - step) % AXES),
            device_id_type=MESH,
        )

    def far_terms(i, carry):
        for j in range(2):
            for f in range(f_tiles):
                rows = slice(f * tile, (f + 1) * tile)
                q[2 * i + j, rows] = prod[f, last_s[f * 8 + 2 * i + j]].astype(jnp.bfloat16)
        far = pt[i, 8:].reshape(8 * unit, f_tiles * tile)
        for j in range(2):
            columns = slice(j * 2 * tile, (j + 1) * 2 * tile)
            block = jnp.dot(far, q[2 * i + j], preferred_element_type=jnp.float32)
            leaf[i, :, :, columns] = block.reshape(8, unit, 2 * tile).astype(jnp.bfloat16)
        for at in range(REDUCE_DEPTH):
            reduce_copy(i, at).start()
        return carry

    lax.fori_loop(0, AXES, far_terms, 0)

    def near_terms(i, carry):
        near = pt[i, :8].reshape(8 * unit, f_tiles * tile)
        for j in range(2):
            columns = slice(j * 2 * tile, (j + 1) * 2 * tile)
            block = jnp.dot(near, q[2 * i + j], preferred_element_type=jnp.float32)
            keep[i, :, :, columns] = block.reshape(8, unit, 2 * tile)
        return carry

    lax.fori_loop(0, AXES, near_terms, 0)

    taken = set()

    def waits(step, low, number):
        found = []
        for at, (earlier, first, length) in enumerate(REDUCE):
            begin = first - BASE[earlier]
            if earlier < step and begin < low + number and low < begin + length and at not in taken:
                taken.add(at)
                found.append(at)
        return found

    def total_of(i, step, low, number):
        value = keep[i, low:low + number]
        for earlier in range(step):
            value = value + got[i, BASE[earlier] + low:BASE[earlier] + low + number].astype(jnp.float32)
        return value.astype(jnp.bfloat16)

    for at, (step, first, number) in enumerate(REDUCE):
        if at < REDUCE_DEPTH:
            continue
        low = 2 ** (AXES - 1 - step) + first - BASE[step]
        needed = waits(step, low, number) if step else []

        def send_on(i, carry, at=at, step=step, first=first, number=number, low=low, needed=needed):
            for other in needed:
                reduce_copy(i, other).wait_recv()
            if step:
                sent[i, first - 8:first - 8 + number] = total_of(i, step, low, number)
            reduce_copy(i, at - REDUCE_DEPTH).wait_send()
            reduce_copy(i, at).start()
            return carry

        lax.fori_loop(0, AXES, send_on, 0)

    empty = jnp.zeros((unit, 2 * tile), jnp.bfloat16)
    for block in (0, 4, 18, 22):
        out_ref[:, block * tile:(block + 2) * tile] = empty
    needed = waits(AXES, 0, 1)
    for i in range(AXES):
        for other in needed:
            reduce_copy(i, other).wait_recv()
        mine = total_of(i, AXES, 0, 1)[0]
        for j in range(2):
            pair = 2 * i + j
            block = pair + 2 if pair < 2 else (pair + 6 if pair < 6 else pair + 10)
            for half in range(2):
                columns = slice((block + 4 * half) * tile, (block + 4 * half + 1) * tile)
                out_ref[:, columns] = mine[:, (2 * j + half) * tile:(2 * j + half + 1) * tile]

    def sent_off(i, carry):
        for at in range(len(GATHER) - GATHER_DEPTH, len(GATHER)):
            gather_copy(i, at).wait_send()
        for at in range(len(REDUCE) - REDUCE_DEPTH, len(REDUCE)):
            reduce_copy(i, at).wait_send()
        return carry

    lax.fori_loop(0, AXES, sent_off, 0)
    for step in range(AXES):
        meta_copy(step).wait_send()
    for side in range(2):
        halo_all(side, halo_send).wait()
        halo_meta(side).wait_send()


def local(a_tiles, a_cols, a_count, p_tiles, p_cols):
    f_tiles, slots, tile, _ = a_tiles.shape
    unit = 64
    hbm, smem = pl.BlockSpec(memory_space=pl.ANY), pl.BlockSpec(memory_space=pltpu.SMEM)
    dma = pltpu.SemaphoreType.DMA
    return pl.pallas_call(
        kernel,
        out_shape=jax.ShapeDtypeStruct((unit, 24 * tile), jnp.bfloat16),
        in_specs=[hbm, smem, smem, hbm, smem],
        out_specs=pl.BlockSpec(memory_space=pltpu.VMEM),
        scratch_shapes=[
            pltpu.VMEM((f_tiles, CUBE + 2, tile, 2 * tile), jnp.bfloat16),
            pltpu.VMEM((CUBE + 2, 8, tile), jnp.int32),
            pltpu.VMEM((f_tiles, slots, tile, tile), jnp.bfloat16),
            pltpu.VMEM((f_tiles, tile, 2 * tile), jnp.bfloat16),
            pltpu.VMEM((f_tiles, 2 * tile, tile), jnp.float32),
            pltpu.VMEM((AXES, CUBE, unit, f_tiles * tile), jnp.bfloat16),
            pltpu.VMEM((f_tiles, slots + 1, tile, 2 * tile), jnp.float32),
            pltpu.VMEM((8, f_tiles * tile, 2 * tile), jnp.bfloat16),
            pltpu.VMEM((AXES, 8, unit, 4 * tile), jnp.float32),
            pltpu.VMEM((AXES, 8, unit, 4 * tile), jnp.bfloat16),
            pltpu.VMEM((AXES, 7, unit, 4 * tile), jnp.bfloat16),
            pltpu.VMEM((AXES, 15, unit, 4 * tile), jnp.bfloat16),
            pltpu.SMEM((CUBE + 2, 8, tile), jnp.int32),
            pltpu.SMEM((4, f_tiles * slots), jnp.int32),
            pltpu.SMEM((f_tiles * slots,), jnp.int32),
            pltpu.SMEM((f_tiles * 8,), jnp.int32),
            dma,
            dma,
            dma,
            dma((AXES, GATHER_DEPTH)),
            dma((AXES, CUBE)),
            dma((AXES,)),
            dma((AXES,)),
            dma((2, 2)),
            dma((2, 2)),
            dma((AXES, REDUCE_DEPTH)),
            dma((AXES, len(REDUCE))),
        ],
        compiler_params=pltpu.CompilerParams(collective_id=0, has_side_effects=True, vmem_limit_bytes=60 * 2 ** 20),
    )(a_tiles, a_cols, a_count, p_tiles, p_cols.T)


def solution(mesh):
    placed = (
        P(("dom", "sub"), None, None, None),
        P(("dom", "sub"), None),
        P(("dom", "sub")),
        P(("dom", "sub"), None, None),
        P(("dom", "sub"), None),
    )
    return jax.shard_map(
        local, mesh=mesh, in_specs=placed, out_specs=P(("dom", "sub"), None), check_vma=False
    )
```

```python
import jax
import jax.numpy as jnp
from jax import lax
from jax.experimental import pallas as pl
from jax.experimental.pallas import tpu as pltpu
from jax.sharding import PartitionSpec as P

MESH = pl.DeviceIdType.MESH

AXES = 4
CUBE = 16
LEFT, RIGHT = CUBE, CUBE + 1
GATHER = [(0, 0), (0, 1), (0, 2), (0, 3), (1, 1), (1, 2), (2, 2), (3, 2), (1, 3), (2, 3), (3, 3),
          (4, 3), (5, 3), (6, 3), (7, 3)]
GATHER_DEPTH = 3
BASE = [0, 8, 12, 14]
REDUCE = [(0, 6, 2), (0, 4, 2), (1, 10, 2), (0, 2, 2), (1, 9, 1), (0, 1, 1), (2, 13, 1), (1, 8, 1), (0, 0, 1),
          (2, 12, 1), (3, 14, 1)]
REDUCE_DEPTH = 2


def cube_bits(x, y):
    return [(x + x // 2) % 2, (y + y // 2) % 2, x // 2, y // 2]


def rotated(rel, part):
    power = (1 + part % 2) * (1 + 3 * (part // 2))
    return rel // power + (rel % power) * (CUBE // power)


def kernel(a_hbm, cols_hbm, count_hbm, p_hbm, pcols_hbm, out_ref, pool, meta, a_ref, turned, pt, prod, q, keep, leaf, sent, got,
           cols, count, pcols, meta_s, where_s, prev_s, last_s,
           scalar_sems, a_sem, p_sem, s_sem, ag_send, ag_recv, meta_send, meta_recv, halo_send, halo_recv, rs_send, rs_recv):
    f_tiles, slots, tile = a_ref.shape[0], a_ref.shape[1], a_ref.shape[2]
    unit = keep.shape[2]
    dom, sub = lax.axis_index("dom"), lax.axis_index("sub")
    doms = lax.axis_size("dom")
    x, y = sub % 4, sub // 4
    bits = cube_bits(x, y)
    xa, xb = x + 1 - 2 * (x % 2), 3 - x
    ya, yb = y + 1 - 2 * (y % 2), 3 - y

    def partner(axis):
        in_x, high = (axis + 1) % 2, axis // 2
        px = in_x * ((1 - high) * xa + high * xb) + (1 - in_x) * x
        py = (1 - in_x) * ((1 - high) * ya + high * yb) + in_x * y
        return (dom, py * 4 + px)

    def away(source):
        theirs = cube_bits(source % 4, source // 4)
        return sum(((bits[axis] + theirs[axis]) % 2) * 2 ** axis for axis in range(AXES))

    after = (lax.rem(dom + 1, doms), sub)
    before = (lax.rem(dom + doms - 1, doms), sub)

    p_copy = pltpu.make_async_copy(p_hbm, pool.at[:, 0], p_sem)
    p_copy.start()
    barrier = pltpu.get_barrier_semaphore()
    for other in [partner(axis) for axis in range(AXES)] + [after, before]:
        pl.semaphore_signal(barrier, inc=1, device_id=other, device_id_type=MESH)
    a_copy = pltpu.make_async_copy(a_hbm, a_ref, a_sem)
    a_copy.start()
    scalar_copies = [pltpu.make_async_copy(source, target, scalar_sems.at[at])
                     for at, (source, target) in enumerate([(pcols_hbm, pcols), (cols_hbm, cols), (count_hbm, count)])]
    for copy in scalar_copies:
        copy.start()

    p_copy.wait()

    pl.semaphore_wait(barrier, 6)

    last, head = away(CUBE - 1), away(0)

    def final_slot(i, at):
        ahead, behind = rotated(last, i), rotated(head, i)
        begin = jnp.where(ahead // 4 == 1, ahead % 4, jnp.where(behind // 4 == 1, behind % 4, 0))
        return 4 + (at - (len(GATHER) - 4) + begin) % 4

    def gather_copy(i, at):
        slot, step = GATHER[at]
        if slot >= 4:
            slot = final_slot(i, at)
        landing = slot + 2 ** step
        return pltpu.make_async_remote_copy(
            src_ref=pool.at[i, slot],
            dst_ref=pool.at[i, landing],
            send_sem=ag_send.at[i, at % GATHER_DEPTH],
            recv_sem=ag_recv.at[i, landing],
            device_id=partner((i + step) % AXES),
            device_id_type=MESH,
        )

    def arrival(i, slot):
        return pltpu.make_async_copy(pool.at[i, slot], pool.at[i, slot], ag_recv.at[i, slot])

    def meta_copy(step):
        return pltpu.make_async_remote_copy(
            src_ref=meta.at[pl.ds(0, 2 ** step)],
            dst_ref=meta.at[pl.ds(2 ** step, 2 ** step)],
            send_sem=meta_send.at[step],
            recv_sem=meta_recv.at[step],
            device_id=partner(step),
            device_id_type=MESH,
        )

    def halo_copy(i, side):
        rel, other = ((last, after), (head, before))[side]
        return pltpu.make_async_remote_copy(
            src_ref=pool.at[i, rotated(rel, i)],
            dst_ref=pool.at[i, CUBE + side],
            send_sem=halo_send.at[0, side],
            recv_sem=halo_recv.at[0, side],
            device_id=other,
            device_id_type=MESH,
        )

    def halo_meta(side):
        rel, other = ((last, after), (head, before))[side]
        return pltpu.make_async_remote_copy(
            src_ref=meta.at[rel],
            dst_ref=meta.at[CUBE + side],
            send_sem=halo_send.at[1, side],
            recv_sem=halo_recv.at[1, side],
            device_id=other,
            device_id_type=MESH,
        )

    def halo_all(side, sems):
        landed = pool.at[:, CUBE + side]
        return pltpu.make_async_copy(landed, landed, sems.at[0, side])

    def place(f, carry):
        for k in range(slots):
            u = cols[f, k] - dom * (CUBE * f_tiles) + f_tiles
            part, at = u % f_tiles, u // f_tiles
            rel = away((at + CUBE - 1) % CUBE)
            turns = [rotated(rel, i) for i in range(AXES)]
            slot = jnp.where(part == 0, turns[0], jnp.where(part == 1, turns[1], jnp.where(part == 2, turns[2], turns[3])))
            is_left, is_right = at == 0, at == CUBE + 1
            where_s[0, f * slots + k] = part
            where_s[1, f * slots + k] = jnp.where(is_left, LEFT, jnp.where(is_right, RIGHT, slot))
            where_s[2, f * slots + k] = jnp.where(is_left, LEFT, jnp.where(is_right, RIGHT, rel))
            where_s[3, f * slots + k] = jnp.where(is_left, -2, jnp.where(is_right, 6, 2))
        return carry

    def turn(f, carry):
        swap = jnp.full((tile, tile), (pcols[0, f] - dom * 8) // 4, jnp.int32) != 0
        first, second = (pool[f, 0, :, half * tile:(half + 1) * tile].astype(jnp.float32) for half in range(2))
        turned[f, :tile] = jnp.where(swap, second, first).T
        turned[f, tile:] = jnp.where(swap, first, second).T
        return carry

    def lay_out(i, carry):
        for f in range(f_tiles):
            pair = jnp.full((unit, tile), pcols[0, f] % 4, jnp.int32)
            for owner in range(CUBE):
                rows = slice((owner // 8) * tile + (owner % 2) * unit, (owner // 8) * tile + (owner % 2 + 1) * unit)
                slot = rotated(away(owner), i)
                value = jnp.where(pair == (owner // 2) % 4, turned[f, rows], 0.0).astype(jnp.bfloat16)
                pt[i, slot, :, f * tile:(f + 1) * tile] = value
        return carry

    def chain(f, carry):
        pairs = []
        for k in range(slots):
            at = f * slots + k
            home = meta_s[where_s[2, at], 0, where_s[0, at]]
            where_s[4, at] = home // 4
            pair = home % 4 + where_s[3, at]
            pairs.append(jnp.where(k < count[f], pair, -1))
        for k in range(slots):
            found = slots
            for earlier in range(k):
                found = jnp.where(pairs[earlier] == pairs[k], earlier, found)
            prev_s[f * slots + k] = jnp.int32(found)
        for pair in range(8):
            found = slots
            for k in range(slots):
                found = jnp.where(pairs[k] == pair, k, found)
            last_s[f * 8 + pair] = found
        return carry

    seen = {0}
    for at, (slot, step) in enumerate(GATHER):
        new = slot if slot not in seen else None
        seen.add(slot)

        def send(i, carry, at=at, new=new):
            if new is not None:
                arrival(i, new).wait()
            if at >= GATHER_DEPTH:
                gather_copy(i, at - GATHER_DEPTH).wait_send()
            gather_copy(i, at).start()
            return carry

        if slot == 4:
            def early(i, carry):
                for late in range(4, 8):
                    arrival(i, late).wait()
                for side, rel in enumerate((last, head)):
                    @pl.when(rotated(rel, i) < 8)
                    def _():
                        halo_copy(i, side).start()
                return carry

            seen.update(range(4, 8))
            lax.fori_loop(0, AXES, early, 0)

            def send(i, carry, at=at):
                gather_copy(i, at - GATHER_DEPTH).wait_send()
                gather_copy(i, at).start()
                return carry

        lax.fori_loop(0, AXES, send, 0)
        if at == 1:
            scalar_copies[0].wait()
            lanes = lax.broadcasted_iota(jnp.int32, meta.shape[1:], 1)
            meta[0] = sum(jnp.where(lanes == f, pcols[0, f] - dom * 8, 0) for f in range(f_tiles))
            meta_copy(0).start()
            lax.fori_loop(0, f_tiles, turn, 0)
        if at == 2:
            lax.fori_loop(0, 2, lay_out, 0)
        if at == 3:
            meta_copy(0).wait_recv()
            meta_copy(1).start()
        if at == 4:
            lax.fori_loop(2, AXES, lay_out, 0)
        if at == 5:
            meta_copy(1).wait_recv()
            meta_copy(2).start()
        if at == 8:
            meta_copy(2).wait_recv()
            meta_copy(3).start()
        if at == 11:
            meta_copy(3).wait_recv()
            for side in range(2):
                halo_meta(side).start()
        if at == 13:
            for side in range(2):
                halo_meta(side).wait_recv()
            to_scalars = pltpu.make_async_copy(meta, meta_s, s_sem)
            to_scalars.start()

    for copy in scalar_copies[1:]:
        copy.wait()
    lax.fori_loop(0, f_tiles, place, 0)
    to_scalars.wait()
    lax.fori_loop(0, f_tiles, chain, 0)
    for f in range(f_tiles):
        prod[f, slots] = jnp.zeros(prod.shape[2:], jnp.float32)

    def late(i, carry):
        for side, rel in enumerate((last, head)):
            mine = rotated(rel, i)

            @pl.when(mine >= 8)
            def _():
                arrival(i, mine).wait()
                halo_copy(i, side).start()
        return carry

    lax.fori_loop(0, AXES, late, 0)

    def rest(i, carry):
        ahead, behind = rotated(last, i), rotated(head, i)
        for slot in range(8, CUBE):
            @pl.when((slot - ahead) * (slot - behind) != 0)
            def _():
                arrival(i, slot).wait()
        return carry

    lax.fori_loop(0, AXES, rest, 0)
    a_copy.wait()

    for side in range(2):
        halo_all(side, halo_recv).wait()

    def multiply(f, carry):
        for k in range(slots):
            at = f * slots + k
            product = jnp.dot(a_ref[f, k], pool[where_s[0, at], where_s[1, at]], preferred_element_type=jnp.float32)
            swap = jnp.full((tile, tile), where_s[4, at], jnp.int32) != 0
            first, second = product[:, :tile], product[:, tile:]
            product = jnp.concatenate([jnp.where(swap, second, first), jnp.where(swap, first, second)], axis=1)
            prod[f, k] = product + prod[f, prev_s[at]] if k else product
        return carry

    lax.fori_loop(0, f_tiles, multiply, 0)

    def reduce_copy(i, at):
        step, first, number = REDUCE[at]
        return pltpu.make_async_remote_copy(
            src_ref=leaf.at[i, pl.ds(first, number)] if step == 0 else sent.at[i, pl.ds(first - 8, number)],
            dst_ref=got.at[i, pl.ds(first, number)],
            send_sem=rs_send.at[i, at % REDUCE_DEPTH],
            recv_sem=rs_recv.at[i, at],
            device_id=partner((i + AXES - 1 - step) % AXES),
            device_id_type=MESH,
        )

    def far_terms(i, carry):
        for j in range(2):
            for f in range(f_tiles):
                rows = slice(f * tile, (f + 1) * tile)
                q[2 * i + j, rows] = prod[f, last_s[f * 8 + 2 * i + j]].astype(jnp.bfloat16)
        far = pt[i, 8:].reshape(8 * unit, f_tiles * tile)
        for j in range(2):
            columns = slice(j * 2 * tile, (j + 1) * 2 * tile)
            block = jnp.dot(far, q[2 * i + j], preferred_element_type=jnp.float32)
            leaf[i, :, :, columns] = block.reshape(8, unit, 2 * tile).astype(jnp.bfloat16)
        for at in range(REDUCE_DEPTH):
            reduce_copy(i, at).start()
        return carry

    lax.fori_loop(0, AXES, far_terms, 0)

    def near_terms(i, carry):
        near = pt[i, :8].reshape(8 * unit, f_tiles * tile)
        for j in range(2):
            columns = slice(j * 2 * tile, (j + 1) * 2 * tile)
            block = jnp.dot(near, q[2 * i + j], preferred_element_type=jnp.float32)
            keep[i, :, :, columns] = block.reshape(8, unit, 2 * tile)
        return carry

    lax.fori_loop(0, AXES, near_terms, 0)

    taken = set()

    def waits(step, low, number):
        found = []
        for at, (earlier, first, length) in enumerate(REDUCE):
            begin = first - BASE[earlier]
            if earlier < step and begin < low + number and low < begin + length and at not in taken:
                taken.add(at)
                found.append(at)
        return found

    def total_of(i, step, low, number):
        value = keep[i, low:low + number]
        for earlier in range(step):
            value = value + got[i, BASE[earlier] + low:BASE[earlier] + low + number].astype(jnp.float32)
        return value.astype(jnp.bfloat16)

    for at, (step, first, number) in enumerate(REDUCE):
        if at < REDUCE_DEPTH:
            continue
        low = 2 ** (AXES - 1 - step) + first - BASE[step]
        needed = waits(step, low, number) if step else []

        def send_on(i, carry, at=at, step=step, first=first, number=number, low=low, needed=needed):
            for other in needed:
                reduce_copy(i, other).wait_recv()
            if step:
                sent[i, first - 8:first - 8 + number] = total_of(i, step, low, number)
            reduce_copy(i, at - REDUCE_DEPTH).wait_send()
            reduce_copy(i, at).start()
            return carry

        lax.fori_loop(0, AXES, send_on, 0)

    empty = jnp.zeros((unit, 2 * tile), jnp.bfloat16)
    for block in (0, 4, 18, 22):
        out_ref[:, block * tile:(block + 2) * tile] = empty
    needed = waits(AXES, 0, 1)
    for i in range(AXES):
        for other in needed:
            reduce_copy(i, other).wait_recv()
        mine = total_of(i, AXES, 0, 1)[0]
        for j in range(2):
            pair = 2 * i + j
            block = pair + 2 if pair < 2 else (pair + 6 if pair < 6 else pair + 10)
            for half in range(2):
                columns = slice((block + 4 * half) * tile, (block + 4 * half + 1) * tile)
                out_ref[:, columns] = mine[:, (2 * j + half) * tile:(2 * j + half + 1) * tile]

    def sent_off(i, carry):
        for at in range(len(GATHER) - GATHER_DEPTH, len(GATHER)):
            gather_copy(i, at).wait_send()
        for at in range(len(REDUCE) - REDUCE_DEPTH, len(REDUCE)):
            reduce_copy(i, at).wait_send()
        return carry

    lax.fori_loop(0, AXES, sent_off, 0)
    for step in range(AXES):
        meta_copy(step).wait_send()
    for side in range(2):
        halo_all(side, halo_send).wait()
        halo_meta(side).wait_send()


def local(a_tiles, a_cols, a_count, p_tiles, p_cols):
    f_tiles, slots, tile, _ = a_tiles.shape
    unit = 64
    hbm = pl.BlockSpec(memory_space=pl.ANY)
    dma = pltpu.SemaphoreType.DMA
    return pl.pallas_call(
        kernel,
        out_shape=jax.ShapeDtypeStruct((unit, 24 * tile), jnp.bfloat16),
        in_specs=[hbm] * 5,
        out_specs=pl.BlockSpec(memory_space=pltpu.VMEM),
        scratch_shapes=[
            pltpu.VMEM((f_tiles, CUBE + 2, tile, 2 * tile), jnp.bfloat16),
            pltpu.VMEM((CUBE + 2, 8, tile), jnp.int32),
            pltpu.VMEM((f_tiles, slots, tile, tile), jnp.bfloat16),
            pltpu.VMEM((f_tiles, 2 * tile, tile), jnp.float32),
            pltpu.VMEM((AXES, CUBE, unit, f_tiles * tile), jnp.bfloat16),
            pltpu.VMEM((f_tiles, slots + 1, tile, 2 * tile), jnp.float32),
            pltpu.VMEM((8, f_tiles * tile, 2 * tile), jnp.bfloat16),
            pltpu.VMEM((AXES, 8, unit, 4 * tile), jnp.float32),
            pltpu.VMEM((AXES, 8, unit, 4 * tile), jnp.bfloat16),
            pltpu.VMEM((AXES, 7, unit, 4 * tile), jnp.bfloat16),
            pltpu.VMEM((AXES, 15, unit, 4 * tile), jnp.bfloat16),
            pltpu.SMEM((f_tiles, slots), jnp.int32),
            pltpu.SMEM((f_tiles,), jnp.int32),
            pltpu.SMEM((2, f_tiles), jnp.int32),
            pltpu.SMEM((CUBE + 2, 8, tile), jnp.int32),
            pltpu.SMEM((5, f_tiles * slots), jnp.int32),
            pltpu.SMEM((f_tiles * slots,), jnp.int32),
            pltpu.SMEM((f_tiles * 8,), jnp.int32),
            dma((3,)),
            dma,
            dma,
            dma,
            dma((AXES, GATHER_DEPTH)),
            dma((AXES, CUBE)),
            dma((AXES,)),
            dma((AXES,)),
            dma((2, 2)),
            dma((2, 2)),
            dma((AXES, REDUCE_DEPTH)),
            dma((AXES, len(REDUCE))),
        ],
        compiler_params=pltpu.CompilerParams(collective_id=0, has_side_effects=True, vmem_limit_bytes=60 * 2 ** 20),
    )(a_tiles, a_cols, a_count, p_tiles, p_cols.T)


def solution(mesh):
    placed = (
        P(("dom", "sub"), None, None, None),
        P(("dom", "sub"), None),
        P(("dom", "sub")),
        P(("dom", "sub"), None, None),
        P(("dom", "sub"), None),
    )
    return jax.shard_map(
        local, mesh=mesh, in_specs=placed, out_specs=P(("dom", "sub"), None), check_vma=False
    )
```

```python
import jax
import jax.numpy as jnp
from jax import lax
from jax.experimental import pallas as pl
from jax.experimental.pallas import tpu as pltpu
from jax.sharding import PartitionSpec as P

MESH = pl.DeviceIdType.MESH

AXES = 4
CUBE = 16
LEFT, RIGHT = CUBE, CUBE + 1
GATHER = [(0, 0), (0, 1), (0, 2), (0, 3), (1, 1), (1, 2), (2, 2), (3, 2), (1, 3), (2, 3), (3, 3),
          (4, 3), (5, 3), (6, 3), (7, 3)]
GATHER_DEPTH = 3
BASE = [0, 8, 12, 14]
REDUCE = [(0, 6, 2), (0, 4, 2), (1, 10, 2), (0, 2, 2), (1, 9, 1), (0, 1, 1), (2, 13, 1), (1, 8, 1), (0, 0, 1),
          (2, 12, 1), (3, 14, 1)]
REDUCE_DEPTH = 2


def cube_bits(x, y):
    return [(x + x // 2) % 2, (y + y // 2) % 2, x // 2, y // 2]


def rotated(rel, part):
    power = (1 + part % 2) * (1 + 3 * (part // 2))
    return rel // power + (rel % power) * (CUBE // power)


def kernel(a_hbm, cols, count, p_hbm, pcols, out_ref, pool, meta, a_ref, p_ref, turned, pt, prod, q, keep, leaf, sent, got,
           meta_s, where_s, prev_s, last_s,
           a_sem, p_sem, s_sem, ag_send, ag_recv, meta_send, meta_recv, halo_send, halo_recv, rs_send, rs_recv):
    f_tiles, slots, tile = a_ref.shape[0], a_ref.shape[1], a_ref.shape[2]
    unit = keep.shape[2]
    dom, sub = lax.axis_index("dom"), lax.axis_index("sub")
    doms = lax.axis_size("dom")
    x, y = sub % 4, sub // 4
    bits = cube_bits(x, y)
    xa, xb = x + 1 - 2 * (x % 2), 3 - x
    ya, yb = y + 1 - 2 * (y % 2), 3 - y

    def partner(axis):
        in_x, high = (axis + 1) % 2, axis // 2
        px = in_x * ((1 - high) * xa + high * xb) + (1 - in_x) * x
        py = (1 - in_x) * ((1 - high) * ya + high * yb) + in_x * y
        return (dom, py * 4 + px)

    def away(source):
        theirs = cube_bits(source % 4, source // 4)
        return sum(((bits[axis] + theirs[axis]) % 2) * 2 ** axis for axis in range(AXES))

    after = (lax.rem(dom + 1, doms), sub)
    before = (lax.rem(dom + doms - 1, doms), sub)

    p_copy = pltpu.make_async_copy(p_hbm, p_ref, p_sem)
    p_copy.start()
    barrier = pltpu.get_barrier_semaphore()
    for other in [partner(axis) for axis in range(AXES)] + [after, before]:
        pl.semaphore_signal(barrier, inc=1, device_id=other, device_id_type=MESH)
    a_copy = pltpu.make_async_copy(a_hbm, a_ref, a_sem)
    a_copy.start()

    lanes = lax.broadcasted_iota(jnp.int32, meta.shape[1:], 1)
    meta[0] = sum(jnp.where(lanes == f, pcols[0, f] % 4, 0) for f in range(f_tiles))
    p_copy.wait()

    def arrange(i, carry):
        high = (pcols[0, i] - dom * 8) // 4
        first = p_ref[i, :, :tile].astype(jnp.float32)
        second = p_ref[i, :, tile:].astype(jnp.float32)
        swap = jnp.full(first.shape, high, jnp.int32) != 0
        pool[i, 0, :, :tile] = jnp.where(swap, second, first).astype(jnp.bfloat16)
        pool[i, 0, :, tile:] = jnp.where(swap, first, second).astype(jnp.bfloat16)
        return carry

    lax.fori_loop(0, f_tiles, arrange, 0)
    pl.semaphore_wait(barrier, 6)

    last, head = away(CUBE - 1), away(0)

    def final_slot(i, at):
        ahead, behind = rotated(last, i), rotated(head, i)
        begin = jnp.where(ahead // 4 == 1, ahead % 4, jnp.where(behind // 4 == 1, behind % 4, 0))
        return 4 + (at - (len(GATHER) - 4) + begin) % 4

    def gather_copy(i, at):
        slot, step = GATHER[at]
        if slot >= 4:
            slot = final_slot(i, at)
        landing = slot + 2 ** step
        return pltpu.make_async_remote_copy(
            src_ref=pool.at[i, slot],
            dst_ref=pool.at[i, landing],
            send_sem=ag_send.at[i, at % GATHER_DEPTH],
            recv_sem=ag_recv.at[i, landing],
            device_id=partner((i + step) % AXES),
            device_id_type=MESH,
        )

    def arrival(i, slot):
        return pltpu.make_async_copy(pool.at[i, slot], pool.at[i, slot], ag_recv.at[i, slot])

    def meta_copy(step):
        return pltpu.make_async_remote_copy(
            src_ref=meta.at[pl.ds(0, 2 ** step)],
            dst_ref=meta.at[pl.ds(2 ** step, 2 ** step)],
            send_sem=meta_send.at[step],
            recv_sem=meta_recv.at[step],
            device_id=partner(step),
            device_id_type=MESH,
        )

    def halo_copy(i, side):
        rel, other = ((last, after), (head, before))[side]
        return pltpu.make_async_remote_copy(
            src_ref=pool.at[i, rotated(rel, i)],
            dst_ref=pool.at[i, CUBE + side],
            send_sem=halo_send.at[0, side],
            recv_sem=halo_recv.at[0, side],
            device_id=other,
            device_id_type=MESH,
        )

    def halo_meta(side):
        rel, other = ((last, after), (head, before))[side]
        return pltpu.make_async_remote_copy(
            src_ref=meta.at[rel],
            dst_ref=meta.at[CUBE + side],
            send_sem=halo_send.at[1, side],
            recv_sem=halo_recv.at[1, side],
            device_id=other,
            device_id_type=MESH,
        )

    def halo_all(side, sems):
        landed = pool.at[:, CUBE + side]
        return pltpu.make_async_copy(landed, landed, sems.at[0, side])

    def place(f, carry):
        for k in range(slots):
            u = cols[f, k] - dom * (CUBE * f_tiles) + f_tiles
            part, at = u % f_tiles, u // f_tiles
            rel = away((at + CUBE - 1) % CUBE)
            turns = [rotated(rel, i) for i in range(AXES)]
            slot = jnp.where(part == 0, turns[0], jnp.where(part == 1, turns[1], jnp.where(part == 2, turns[2], turns[3])))
            is_left, is_right = at == 0, at == CUBE + 1
            where_s[0, f * slots + k] = part
            where_s[1, f * slots + k] = jnp.where(is_left, LEFT, jnp.where(is_right, RIGHT, slot))
            where_s[2, f * slots + k] = jnp.where(is_left, LEFT, jnp.where(is_right, RIGHT, rel))
            where_s[3, f * slots + k] = jnp.where(is_left, -2, jnp.where(is_right, 6, 2))
        return carry

    def turn(f, carry):
        turned[f] = pool[f, 0].astype(jnp.float32).T
        return carry

    def lay_out(i, carry):
        for f in range(f_tiles):
            pair = jnp.full((unit, tile), pcols[0, f] % 4, jnp.int32)
            for owner in range(CUBE):
                rows = slice((owner // 8) * tile + (owner % 2) * unit, (owner // 8) * tile + (owner % 2 + 1) * unit)
                slot = rotated(away(owner), i)
                value = jnp.where(pair == (owner // 2) % 4, turned[f, rows], 0.0).astype(jnp.bfloat16)
                pt[i, slot, :, f * tile:(f + 1) * tile] = value
        return carry

    def chain(f, carry):
        pairs = []
        for k in range(slots):
            at = f * slots + k
            pair = meta_s[where_s[2, at], 0, where_s[0, at]] + where_s[3, at]
            pairs.append(jnp.where(k < count[f], pair, -1))
        for k in range(slots):
            found = slots
            for earlier in range(k):
                found = jnp.where(pairs[earlier] == pairs[k], earlier, found)
            prev_s[f * slots + k] = jnp.int32(found)
        for pair in range(8):
            found = slots
            for k in range(slots):
                found = jnp.where(pairs[k] == pair, k, found)
            last_s[f * 8 + pair] = found
        return carry

    meta_copy(0).start()
    seen = {0}
    for at, (slot, step) in enumerate(GATHER):
        new = slot if slot not in seen else None
        seen.add(slot)

        def send(i, carry, at=at, new=new):
            if new is not None:
                arrival(i, new).wait()
            if at >= GATHER_DEPTH:
                gather_copy(i, at - GATHER_DEPTH).wait_send()
            gather_copy(i, at).start()
            return carry

        if slot == 4:
            def early(i, carry):
                for late in range(4, 8):
                    arrival(i, late).wait()
                for side, rel in enumerate((last, head)):
                    @pl.when(rotated(rel, i) < 8)
                    def _():
                        halo_copy(i, side).start()
                return carry

            seen.update(range(4, 8))
            lax.fori_loop(0, AXES, early, 0)

            def send(i, carry, at=at):
                gather_copy(i, at - GATHER_DEPTH).wait_send()
                gather_copy(i, at).start()
                return carry

        lax.fori_loop(0, AXES, send, 0)
        if at == 1:
            lax.fori_loop(0, f_tiles, turn, 0)
        if at == 2:
            lax.fori_loop(0, 2, lay_out, 0)
        if at == 3:
            meta_copy(0).wait_recv()
            meta_copy(1).start()
        if at == 4:
            lax.fori_loop(2, AXES, lay_out, 0)
        if at == 5:
            meta_copy(1).wait_recv()
            meta_copy(2).start()
        if at == 8:
            meta_copy(2).wait_recv()
            meta_copy(3).start()
        if at == 11:
            meta_copy(3).wait_recv()
            for side in range(2):
                halo_meta(side).start()
        if at == 13:
            for side in range(2):
                halo_meta(side).wait_recv()
            to_scalars = pltpu.make_async_copy(meta, meta_s, s_sem)
            to_scalars.start()

    lax.fori_loop(0, f_tiles, place, 0)
    to_scalars.wait()
    lax.fori_loop(0, f_tiles, chain, 0)
    for f in range(f_tiles):
        prod[f, slots] = jnp.zeros(prod.shape[2:], jnp.float32)

    def late(i, carry):
        for side, rel in enumerate((last, head)):
            mine = rotated(rel, i)

            @pl.when(mine >= 8)
            def _():
                arrival(i, mine).wait()
                halo_copy(i, side).start()
        return carry

    lax.fori_loop(0, AXES, late, 0)

    def rest(i, carry):
        ahead, behind = rotated(last, i), rotated(head, i)
        for slot in range(8, CUBE):
            @pl.when((slot - ahead) * (slot - behind) != 0)
            def _():
                arrival(i, slot).wait()
        return carry

    lax.fori_loop(0, AXES, rest, 0)
    a_copy.wait()

    for side in range(2):
        halo_all(side, halo_recv).wait()

    def multiply(f, carry):
        for k in range(slots):
            at = f * slots + k
            product = jnp.dot(a_ref[f, k], pool[where_s[0, at], where_s[1, at]], preferred_element_type=jnp.float32)
            prod[f, k] = product + prod[f, prev_s[at]] if k else product
        return carry

    lax.fori_loop(0, f_tiles, multiply, 0)

    def reduce_copy(i, at):
        step, first, number = REDUCE[at]
        return pltpu.make_async_remote_copy(
            src_ref=leaf.at[i, pl.ds(first, number)] if step == 0 else sent.at[i, pl.ds(first - 8, number)],
            dst_ref=got.at[i, pl.ds(first, number)],
            send_sem=rs_send.at[i, at % REDUCE_DEPTH],
            recv_sem=rs_recv.at[i, at],
            device_id=partner((i + AXES - 1 - step) % AXES),
            device_id_type=MESH,
        )

    def far_terms(i, carry):
        for j in range(2):
            for f in range(f_tiles):
                rows = slice(f * tile, (f + 1) * tile)
                q[2 * i + j, rows] = prod[f, last_s[f * 8 + 2 * i + j]].astype(jnp.bfloat16)
        far = pt[i, 8:].reshape(8 * unit, f_tiles * tile)
        for j in range(2):
            columns = slice(j * 2 * tile, (j + 1) * 2 * tile)
            block = jnp.dot(far, q[2 * i + j], preferred_element_type=jnp.float32)
            leaf[i, :, :, columns] = block.reshape(8, unit, 2 * tile).astype(jnp.bfloat16)
        for at in range(REDUCE_DEPTH):
            reduce_copy(i, at).start()
        return carry

    lax.fori_loop(0, AXES, far_terms, 0)

    def near_terms(i, carry):
        near = pt[i, :8].reshape(8 * unit, f_tiles * tile)
        for j in range(2):
            columns = slice(j * 2 * tile, (j + 1) * 2 * tile)
            block = jnp.dot(near, q[2 * i + j], preferred_element_type=jnp.float32)
            keep[i, :, :, columns] = block.reshape(8, unit, 2 * tile)
        return carry

    lax.fori_loop(0, AXES, near_terms, 0)

    taken = set()

    def waits(step, low, number):
        found = []
        for at, (earlier, first, length) in enumerate(REDUCE):
            begin = first - BASE[earlier]
            if earlier < step and begin < low + number and low < begin + length and at not in taken:
                taken.add(at)
                found.append(at)
        return found

    def total_of(i, step, low, number):
        value = keep[i, low:low + number]
        for earlier in range(step):
            value = value + got[i, BASE[earlier] + low:BASE[earlier] + low + number].astype(jnp.float32)
        return value.astype(jnp.bfloat16)

    for at, (step, first, number) in enumerate(REDUCE):
        if at < REDUCE_DEPTH:
            continue
        low = 2 ** (AXES - 1 - step) + first - BASE[step]
        needed = waits(step, low, number) if step else []

        def send_on(i, carry, at=at, step=step, first=first, number=number, low=low, needed=needed):
            for other in needed:
                reduce_copy(i, other).wait_recv()
            if step:
                sent[i, first - 8:first - 8 + number] = total_of(i, step, low, number)
            reduce_copy(i, at - REDUCE_DEPTH).wait_send()
            reduce_copy(i, at).start()
            return carry

        lax.fori_loop(0, AXES, send_on, 0)

    empty = jnp.zeros((unit, 2 * tile), jnp.bfloat16)
    for block in (0, 4, 18, 22):
        out_ref[:, block * tile:(block + 2) * tile] = empty
    needed = waits(AXES, 0, 1)
    for i in range(AXES):
        for other in needed:
            reduce_copy(i, other).wait_recv()
        mine = total_of(i, AXES, 0, 1)[0]
        for j in range(2):
            pair = 2 * i + j
            block = pair + 2 if pair < 2 else (pair + 6 if pair < 6 else pair + 10)
            for half in range(2):
                columns = slice((block + 4 * half) * tile, (block + 4 * half + 1) * tile)
                out_ref[:, columns] = mine[:, (2 * j + half) * tile:(2 * j + half + 1) * tile]

    def sent_off(i, carry):
        for at in range(len(GATHER) - GATHER_DEPTH, len(GATHER)):
            gather_copy(i, at).wait_send()
        for at in range(len(REDUCE) - REDUCE_DEPTH, len(REDUCE)):
            reduce_copy(i, at).wait_send()
        return carry

    lax.fori_loop(0, AXES, sent_off, 0)
    for step in range(AXES):
        meta_copy(step).wait_send()
    for side in range(2):
        halo_all(side, halo_send).wait()
        halo_meta(side).wait_send()


def local(a_tiles, a_cols, a_count, p_tiles, p_cols):
    f_tiles, slots, tile, _ = a_tiles.shape
    unit = 64
    hbm, smem = pl.BlockSpec(memory_space=pl.ANY), pl.BlockSpec(memory_space=pltpu.SMEM)
    dma = pltpu.SemaphoreType.DMA
    return pl.pallas_call(
        kernel,
        out_shape=jax.ShapeDtypeStruct((unit, 24 * tile), jnp.bfloat16),
        in_specs=[hbm, smem, smem, hbm, smem],
        out_specs=pl.BlockSpec(memory_space=pltpu.VMEM),
        scratch_shapes=[
            pltpu.VMEM((f_tiles, CUBE + 2, tile, 2 * tile), jnp.bfloat16),
            pltpu.VMEM((CUBE + 2, 8, tile), jnp.int32),
            pltpu.VMEM((f_tiles, slots, tile, tile), jnp.bfloat16),
            pltpu.VMEM((f_tiles, tile, 2 * tile), jnp.bfloat16),
            pltpu.VMEM((f_tiles, 2 * tile, tile), jnp.float32),
            pltpu.VMEM((AXES, CUBE, unit, f_tiles * tile), jnp.bfloat16),
            pltpu.VMEM((f_tiles, slots + 1, tile, 2 * tile), jnp.float32),
            pltpu.VMEM((8, f_tiles * tile, 2 * tile), jnp.bfloat16),
            pltpu.VMEM((AXES, 8, unit, 4 * tile), jnp.float32),
            pltpu.VMEM((AXES, 8, unit, 4 * tile), jnp.bfloat16),
            pltpu.VMEM((AXES, 7, unit, 4 * tile), jnp.bfloat16),
            pltpu.VMEM((AXES, 15, unit, 4 * tile), jnp.bfloat16),
            pltpu.SMEM((CUBE + 2, 8, tile), jnp.int32),
            pltpu.SMEM((4, f_tiles * slots), jnp.int32),
            pltpu.SMEM((f_tiles * slots,), jnp.int32),
            pltpu.SMEM((f_tiles * 8,), jnp.int32),
            dma,
            dma,
            dma,
            dma((AXES, GATHER_DEPTH)),
            dma((AXES, CUBE)),
            dma((AXES,)),
            dma((AXES,)),
            dma((2, 2)),
            dma((2, 2)),
            dma((AXES, REDUCE_DEPTH)),
            dma((AXES, len(REDUCE))),
        ],
        compiler_params=pltpu.CompilerParams(collective_id=0, has_side_effects=True, vmem_limit_bytes=60 * 2 ** 20),
    )(a_tiles, a_cols, a_count, p_tiles, p_cols.T)


def solution(mesh):
    placed = (
        P(("dom", "sub"), None, None, None),
        P(("dom", "sub"), None),
        P(("dom", "sub")),
        P(("dom", "sub"), None, None),
        P(("dom", "sub"), None),
    )
    return jax.shard_map(
        local, mesh=mesh, in_specs=placed, out_specs=P(("dom", "sub"), None), check_vma=False
    )
```
